32 devices in a mesh: outer: 8 (over y, x, core), node: 4 (over z).
Axes of the slice: x: 2, y: 2, z: 4, core: 2. Of those that a mesh axis runs over, the one named last changes fastest.
Arguments:
- context: bfloat16 [2048, 4096], P('outer', 'node'), may hold values from -6 to 6
- grad_out: bfloat16 [2048, 4096], P('outer', 'node'), may hold values from -6 to 6
- out_weight: bfloat16 [4096, 4096], P('node', 'outer'), may hold values from -0.09375 to 0.09375
Outputs:
- context_grad: bfloat16 [2048, 4096], P('outer', 'node')
- weight_grad: float32 [4096, 4096], P('node', 'outer')
The draws below stay inside these ranges and needn't reach their ends.
All inputs are finite; a program needn't handle non-finite values.
Results may differ from the reference program's by a relative error of at most 0.001.
Values may be sent and summed in bfloat16 or wider, within the bound.
No kernel may reach another device: no remote copies, remote signals or barrier semaphores. Data moves between devices by JAX's collectives and lax.ppermute only.
A program may use at most 64 MiB of HBM per device.

```python
import math
import jax
import jax.numpy as jnp
from jax import lax

D_IN = 4096
DM = 4096
TOKENS = 2048


def level_of(stream_key, dims, split, least, largest):
    def one(dim, blocks):
        heights = jax.random.uniform(jax.random.fold_in(jax.random.fold_in(stream_key, 6), dim), (blocks,), jnp.float32, least / len(split), largest / len(split))
        return jnp.repeat(jnp.exp(heights), dims[dim] // blocks).reshape((-1,) + (1,) * (len(dims) - dim - 1))

    gain = one(*split[0])
    for cut in split[1:]:
        gain = gain * one(*cut)
    return gain


def centred(rng, dims, scale, bound, cuts=(), kind=jnp.bfloat16):
    loudness = level_of(rng, dims, cuts, -0.22, 0.18) if cuts else 1.0
    values = jax.random.normal(rng, dims, jnp.float32) * scale * loudness
    return jnp.minimum(jnp.maximum(values, -bound), bound).astype(kind)


def setup_inputs(seed: int = 0) -> dict:
    key_list = jax.random.split(jax.random.key(seed), 4)
    return {
        "context": centred(key_list[0], (TOKENS, D_IN), 1.0, 6.0, ((0, 8), (1, 4))),
        "grad_out": centred(key_list[1], (TOKENS, DM), 1.0, 6.0, ((0, 8), (1, 4))),
        "out_weight": centred(key_list[2], (D_IN, DM), D_IN ** -0.5, 0.09375, ((0, 4), (1, 8))),
    }


def reference(context, grad_out, out_weight):
    context_grad = lax.dot_general(grad_out, out_weight, (((1,), (1,)), ((), ())), preferred_element_type=jnp.float32).astype(jnp.bfloat16)
    weight_grad = lax.dot_general(context, grad_out, (((0,), (0,)), ((), ())), preferred_element_type=jnp.float32)
    weight_grad = weight_grad * (1.0 / math.sqrt(TOKENS))
    return (context_grad, weight_grad)
```

```python
import math

import jax
import jax.numpy as jnp
from jax import lax
from jax.sharding import PartitionSpec as P


def plane_of(outer):
    cores = 2 if outer % 2 == 0 else 1
    chips = outer // cores
    cols = max(d for d in range(1, math.isqrt(chips) + 1) if chips % d == 0)
    return chips // cols, cols, cores


def shift(array, db, da, dc):
    outer = lax.axis_size("outer")
    rows, cols, cores = plane_of(outer)

    def source(o):
        b, a, c = o // (cols * cores), o // cores % cols, o % cores
        return ((b + db) % rows * cols + (a + da) % cols) * cores + (c + dc) % cores

    return lax.ppermute(array, "outer", [(source(o), o) for o in range(outer)])


def halves(array, axis):
    half = array.shape[axis] // 2
    return [lax.slice_in_dim(array, 0, half, axis=axis), lax.slice_in_dim(array, half, 2 * half, axis=axis)]


def gather(array, axis):
    rows, cols, cores = plane_of(lax.axis_size("outer"))
    first, second = halves(array, axis)
    got = {(0, 0): [first, second]}
    for da in range(1, cols):
        got[0, da] = [shift(first, 0, da, 0), shift(second, 0, da, 0)]
    for db in range(1, rows):
        got[db, 0] = [shift(first, db, 0, 0), shift(second, db, 0, 0)]
    for db in range(1, rows):
        for da in range(1, cols):
            got[db, da] = [shift(got[0, da][0], db, 0, 0), shift(got[db, 0][1], 0, da, 0)]
    out = {}
    for (db, da), pair in got.items():
        out[db, da, 0] = pair
        for dc in range(1, cores):
            out[db, da, dc] = [shift(piece, 0, 0, dc) for piece in pair]
    return out


def position(db, da, dc):
    rows, cols, cores = plane_of(lax.axis_size("outer"))
    o = lax.axis_index("outer")
    b, a, c = o // (cols * cores), o // cores % cols, o % cores
    return ((b + db) % rows * cols + (a + da) % cols) * cores + (c + dc) % cores


def ring(array):
    node = lax.axis_size("node")
    me = lax.axis_index("node")
    blocks = {0: array}
    up, down = array, array
    for step in range(1, node // 2 + 1):
        up = lax.ppermute(up, "node", [(i, (i + 1) % node) for i in range(node)])
        blocks[node - step] = up
        if 2 * step < node:
            down = lax.ppermute(down, "node", [((i + 1) % node, i) for i in range(node)])
            blocks[step] = down
    whole = jnp.zeros((node,) + array.shape, array.dtype)
    for d, block in blocks.items():
        whole = lax.dynamic_update_index_in_dim(whole, block, (me + d) % node, 0)
    return whole


def body(context, grad_out, out_weight):
    outer = lax.axis_size("outer")
    rows, cols, cores = plane_of(outer)
    tokens = grad_out.shape[0]
    width = out_weight.shape[1]
    norm_scale = 1.0 / math.sqrt(tokens * outer)

    grad = ring(grad_out)
    per = grad_out.shape[1] // width

    def columns(first, count):
        if per:
            block = lax.dynamic_slice(grad, (first // (per * width), 0, first % (per * width)), (1, tokens, count))
            return block.reshape(tokens, count)
        wide = grad.transpose(1, 0, 2).reshape(tokens, -1)
        return lax.dynamic_slice_in_dim(wide, first, count, axis=1)

    weights = gather(out_weight, 1)
    contexts = gather(context, 0)

    context_grad = 0.0
    weight_grad = 0.0
    for at, pair in weights.items():
        half = width // 2
        for h, piece in enumerate(pair):
            context_grad += lax.dot_general(
                columns(position(*at) * width + h * half, half),
                piece,
                (((1,), (1,)), ((), ())),
                preferred_element_type=jnp.float32,
            )
    for at, pair in contexts.items():
        back = (-at[0] % rows, -at[1] % cols, -at[2] % cores)
        mine = columns(position(*back) * width, width)
        theirs = mine if at == (0, 0, 0) else shift(mine, *at)
        half = tokens // 2
        for h, piece in enumerate(pair):
            weight_grad += lax.dot_general(
                piece,
                theirs[h * half : (h + 1) * half],
                (((0,), (0,)), ((), ())),
                preferred_element_type=jnp.float32,
            )
    return (context_grad.astype(jnp.bfloat16), weight_grad * norm_scale)


def solution(mesh):
    in_specs = (P("outer", "node"), P("outer", "node"), P("node", "outer"))
    out_specs = (P("outer", "node"), P("node", "outer"))
    return jax.shard_map(body, mesh=mesh, in_specs=in_specs, out_specs=out_specs, check_vma=False)
```

```python
import math

import jax
import jax.numpy as jnp
from jax import lax
from jax.sharding import PartitionSpec as P


def plane_of(outer):
    cores = 2 if outer % 2 == 0 else 1
    chips = outer // cores
    cols = max(d for d in range(1, math.isqrt(chips) + 1) if chips % d == 0)
    return chips // cols, cols, cores


def place(o, db, da, dc):
    rows, cols, cores = plane_of(lax.axis_size("outer"))
    b, a, c = o // (cols * cores), o // cores % cols, o % cores
    return ((b + db) % rows * cols + (a + da) % cols) * cores + (c + dc) % cores


def shift(array, db, da, dc=0):
    return lax.ppermute(array, "outer", [(place(o, db, da, dc), o) for o in range(lax.axis_size("outer"))])


def split(array, axis):
    half = array.shape[axis] // 2
    return [lax.slice_in_dim(array, 0, half, axis=axis), lax.slice_in_dim(array, half, 2 * half, axis=axis)]


def gather(array, axis):
    rows, cols, _ = plane_of(lax.axis_size("outer"))
    got = {(0, 0): [array]}
    for da in range(1, cols):
        got[0, da] = [shift(array, 0, da)]
    for db in range(1, rows):
        got[db, 0] = [shift(array, db, 0)]
    for db in range(1, rows):
        for da in range(1, cols):
            got[db, da] = [
                shift(split(got[0, da][0], axis)[0], db, 0),
                shift(split(got[db, 0][0], axis)[1], 0, da),
            ]
    return got


def ring(array):
    node = lax.axis_size("node")
    blocks = {0: array}
    up, down = array, array
    for step in range(1, node // 2 + 1):
        up = lax.ppermute(up, "node", [(i, (i + 1) % node) for i in range(node)])
        blocks[node - step] = up
        if 2 * step < node:
            down = lax.ppermute(down, "node", [((i + 1) % node, i) for i in range(node)])
            blocks[step] = down
    return blocks


def stacked(blocks):
    node, me = lax.axis_size("node"), lax.axis_index("node")
    whole = jnp.zeros((node,) + blocks[0].shape, blocks[0].dtype)
    for d, block in blocks.items():
        whole = lax.dynamic_update_index_in_dim(whole, block, (me + d) % node, 0)
    return whole


def body(context, grad_out, out_weight):
    outer, node = lax.axis_size("outer"), lax.axis_size("node")
    rows, cols, cores = plane_of(outer)
    tokens, held = grad_out.shape
    width = out_weight.shape[1]
    norm_scale = 1.0 / math.sqrt(tokens * outer)
    o, z = lax.axis_index("outer"), lax.axis_index("node")
    c = o % cores

    weights = gather(out_weight, 1)
    contexts = gather(context, 0)
    grad = stacked(ring(grad_out))

    def columns(o):
        first = o * width
        if held % width == 0:
            return lax.dynamic_slice(grad, (first // held, 0, first % held), (1, tokens, width))[0]
        return lax.dynamic_slice_in_dim(grad.transpose(1, 0, 2).reshape(tokens, -1), first, width, axis=1)

    def of_kind(kind):
        return jnp.stack([columns(chip * cores + kind) for chip in range(rows * cols)])

    mine = of_kind(c)
    if cores > 1:
        mine = jnp.concatenate([mine, shift(of_kind((c + 1) % cores), 0, 0, 1)], axis=1)
    context_grad = 0.0
    for at, pieces in weights.items():
        chip = place(o, *at, 0) // cores
        block = lax.dynamic_index_in_dim(mine, chip, 0, keepdims=False)
        part = width // len(pieces)
        for h, piece in enumerate(pieces):
            context_grad += lax.dot_general(
                block[:, h * part : (h + 1) * part], piece, (((1,), (1,)), ((), ())), preferred_element_type=jnp.float32
            )
    if cores > 1:
        context_grad = context_grad[:tokens] + shift(context_grad[tokens:], 0, 0, 1)

    def for_chip(db, da):
        return jnp.concatenate([columns(place(o, db, da, dc)) for dc in range(cores)], axis=1)

    weight_grad = 0.0
    for at, pieces in contexts.items():
        db, da = at
        sent = for_chip(-db, -da)
        if db and da and tokens % node == 0:
            part = tokens // node
            share = shift(lax.dynamic_slice_in_dim(sent, z * part, part, axis=0), db, da)
            block = stacked(ring(share)).reshape(tokens, -1)
        else:
            block = shift(sent, db, da) if db or da else sent
        part = tokens // len(pieces)
        for h, piece in enumerate(pieces):
            weight_grad += lax.dot_general(
                piece, block[h * part : (h + 1) * part], (((0,), (0,)), ((), ())), preferred_element_type=jnp.float32
            )
    if cores > 1:
        weight_grad = weight_grad[:, :width] + shift(weight_grad[:, width:], 0, 0, 1)
    return (context_grad.astype(jnp.bfloat16), weight_grad * norm_scale)


def solution(mesh):
    in_specs = (P("outer", "node"), P("outer", "node"), P("node", "outer"))
    out_specs = (P("outer", "node"), P("node", "outer"))
    return jax.shard_map(body, mesh=mesh, in_specs=in_specs, out_specs=out_specs, check_vma=False)
```

```python
import functools
import math

import jax
import jax.numpy as jnp
from jax import lax
from jax.experimental import pallas as pl
from jax.experimental.pallas import tpu as pltpu
from jax.sharding import PartitionSpec as P


def plane_of(outer):
    cores = 2 if outer % 2 == 0 else 1
    chips = outer // cores
    cols = max(d for d in range(1, math.isqrt(chips) + 1) if chips % d == 0)
    return chips // cols, cols, cores


def place(o, db, da, dc):
    rows, cols, cores = plane_of(lax.axis_size("outer"))
    b, a, c = o // (cols * cores), o // cores % cols, o % cores
    return ((b + db) % rows * cols + (a + da) % cols) * cores + (c + dc) % cores


def shift(array, db, da, dc=0):
    return lax.ppermute(array, "outer", [(place(o, db, da, dc), o) for o in range(lax.axis_size("outer"))])


def sibling(array):
    return shift(array, 0, 0, 1)


def along_node(array, d):
    node = lax.axis_size("node")
    return lax.ppermute(array, "node", [((i + d) % node, i) for i in range(node)])


def after(arrays, done):
    return lax.optimization_barrier((arrays, done))[0]


def ring(array):
    node = lax.axis_size("node")
    blocks = {0: array}
    up, down = array, array
    for step in range(1, node // 2 + 1):
        up = along_node(up, -1)
        blocks[node - step] = up
        if 2 * step < node:
            down = along_node(down, 1)
            blocks[step] = down
    return blocks


def stacked(blocks):
    node, me = lax.axis_size("node"), lax.axis_index("node")
    whole = jnp.zeros((node,) + blocks[0].shape, blocks[0].dtype)
    for d, block in blocks.items():
        whole = lax.dynamic_update_index_in_dim(whole, block, (me + d) % node, 0)
    return whole


def pack_kernel(weight, context, out):
    taken, width = weight.shape
    tokens = context.shape[0]
    half = taken // 2
    out[:half] = weight[:half]
    for i in range(taken // width):
        out[half + i * tokens : half + (i + 1) * tokens] = context[:, i * width : (i + 1) * width]
    out[-half:] = weight[half:]


def packed(weight, context):
    taken, width = weight.shape
    high = taken + taken // width * context.shape[0]
    return pl.pallas_call(
        pack_kernel,
        out_shape=jax.ShapeDtypeStruct((high, width), weight.dtype),
        in_specs=[pl.BlockSpec(memory_space=pltpu.VMEM)] * 2,
        out_specs=pl.BlockSpec(memory_space=pltpu.VMEM),
        compiler_params=pltpu.CompilerParams(vmem_limit_bytes=16 * 2**20),
        cost_estimate=pl.CostEstimate(flops=0, bytes_accessed=4 * high * width, transcendentals=0),
    )(weight, context)


def body(context, grad_out, out_weight):
    outer, node = lax.axis_size("outer"), lax.axis_size("node")
    rows, cols, cores = plane_of(outer)
    tokens, held = grad_out.shape
    taken, width = out_weight.shape
    norm_scale = 1.0 / math.sqrt(tokens * outer)
    o, z = lax.axis_index("outer"), lax.axis_index("node")
    c = o % cores
    row = [(0, da) for da in range(1, cols)]
    column = [(db, 0) for db in range(1, rows)]
    across = [(db, da) for db in range(1, rows) for da in range(1, cols)]
    half, slabs = taken // 2, taken // width
    high = taken + slabs * tokens

    def dot(left, right, dim):
        return lax.dot_general(left, right, (((dim,), (dim,)), ((), ())), preferred_element_type=jnp.float32)

    def both(array):
        return [array, sibling(array)] if cores > 1 else [array]

    def wide(slab):
        return jnp.concatenate([slab[i * tokens : (i + 1) * tokens] for i in range(slabs)], axis=1)

    around = ring(grad_out)
    pack = packed(out_weight, context)
    packs = {at: shift(pack, *at) for at in row + column}
    contexts = {(0, 0): both(context)}
    grad = stacked(around)

    def columns(o):
        first = o * width
        if held % width == 0:
            return lax.dynamic_slice(grad, (first // held, 0, first % held), (1, tokens, width))[0]
        return lax.dynamic_slice_in_dim(grad.transpose(1, 0, 2).reshape(tokens, -1), first, width, axis=1)

    def of_kind(kind):
        return jnp.stack([columns(chip * cores + kind) for chip in range(rows * cols)])

    def for_chip(db, da):
        return jnp.concatenate([columns(place(o, db, da, dc)) for dc in range(cores)], axis=1)

    upper = {(db, da): shift(packs[0, da][: high // 2], db, 0) for db, da in across}
    lower = {(db, da): shift(packs[db, 0][high // 2 :], 0, da) for db, da in across}

    pair = 2 if node % 2 == 0 else 1
    part = tokens // pair
    shares = {
        (db, da): lax.dynamic_slice_in_dim(for_chip(-db, -da), z % pair * part, part, axis=0) for db, da in across
    }
    shares = {at: shift(share, *at) for at, share in after(shares, packs).items()}
    mine = of_kind(c)
    if cores > 1:
        mine = jnp.concatenate([mine, sibling(after(of_kind((c + 1) % cores), packs))], axis=1)
    sent = {(db, da): for_chip(-db, -da) for db, da in row + column}
    blocks = {at: shift(block, *at) for at, block in after(sent, (shares, mine)).items()}
    for at, share in shares.items():
        if pair > 1:
            other = lax.ppermute(share, "node", [(i ^ 1, i) for i in range(node)])
            share = jnp.where(z % 2 == 0, jnp.concatenate([share, other]), jnp.concatenate([other, share]))
        blocks[at] = share
    near = jnp.stack([wide(packs[at][half : half + slabs * tokens]) for at in row + column])
    for at, pair in zip(row + column, zip(*both(after(near, [blocks[at] for at in across])))):
        contexts[at] = pair
    for at in across:
        contexts[at] = both(wide(jnp.concatenate([upper[at][half:], lower[at][: high // 2 - half]], axis=0)))

    sides = []
    weights = {(0, 0): (out_weight[:half], out_weight[half:])}
    weights |= {at: (packs[at][:half], packs[at][-half:]) for at in row + column}
    weights |= {at: (upper[at][:half], lower[at][-half:]) for at in across}
    for h in range(2):
        side = 0.0
        for at, pair in weights.items():
            side += dot(lax.dynamic_index_in_dim(mine, place(o, *at, 0) // cores, 0, keepdims=False), pair[h], 1)
        sides.append(side)
    context_grad = jnp.concatenate([side[:tokens] for side in sides], axis=1)
    if cores > 1:
        theirs = jnp.concatenate([side[tokens:] for side in sides], axis=1)
        blocks |= after({at: blocks[at] for at in row + column}, theirs)
        context_grad += sibling(theirs)

    own = lax.dynamic_index_in_dim(mine, o // cores, 0, keepdims=False)
    cotangents = {(0, 0): [own[i * tokens : (i + 1) * tokens] for i in range(cores)]}
    for at in across + row + column:
        cotangents[at] = [blocks[at][:, :width]]
        if cores > 1:
            cotangents[at].append(sibling(blocks[at][:, width:]))
    weight_grad = 0.0
    for group in ([(0, 0)], across, row + column):
        if group:
            left = jnp.concatenate([x for at in group for x in contexts[at]], axis=0)
            right = jnp.concatenate([x for at in group for x in cotangents[at]], axis=0)
            weight_grad += dot(left, right, 0)
    return (context_grad.astype(jnp.bfloat16), weight_grad * norm_scale)


def solution(mesh):
    in_specs = (P("outer", "node"), P("outer", "node"), P("node", "outer"))
    out_specs = (P("outer", "node"), P("node", "outer"))
    return jax.shard_map(body, mesh=mesh, in_specs=in_specs, out_specs=out_specs, check_vma=False)
```

```python
import functools
import math

import jax
import jax.numpy as jnp
from jax import lax
from jax.experimental import pallas as pl
from jax.experimental.pallas import tpu as pltpu
from jax.sharding import PartitionSpec as P

F32, BF16 = jnp.float32, jnp.bfloat16
VMEM = pl.BlockSpec(memory_space=pltpu.VMEM)


def plane_of(outer):
    cores = 2 if outer % 2 == 0 else 1
    chips = outer // cores
    cols = max(d for d in range(1, math.isqrt(chips) + 1) if chips % d == 0)
    return chips // cols, cols, cores


def place(o, db, da, dc):
    rows, cols, cores = plane_of(lax.axis_size("outer"))
    b, a, c = o // (cols * cores), o // cores % cols, o % cores
    return ((b + db) % rows * cols + (a + da) % cols) * cores + (c + dc) % cores


def chip_at(db, da):
    rows, cols, cores = plane_of(lax.axis_size("outer"))
    chip = lax.div(lax.axis_index("outer"), jnp.int32(cores))
    b, a = lax.div(chip, jnp.int32(cols)), lax.rem(chip, jnp.int32(cols))
    return lax.rem(b + db % rows, jnp.int32(rows)) * cols + lax.rem(a + da % cols, jnp.int32(cols))


def kind_at(dc):
    cores = plane_of(lax.axis_size("outer"))[2]
    return lax.rem(lax.axis_index("outer") + dc, jnp.int32(cores))


def shift(array, db, da, dc=0):
    return lax.ppermute(array, "outer", [(place(o, db, da, dc), o) for o in range(lax.axis_size("outer"))])


def sibling(array):
    return shift(array, 0, 0, 1)


def along_node(array, d):
    node = lax.axis_size("node")
    return lax.ppermute(array, "node", [((i + d) % node, i) for i in range(node)])


def after(arrays, done):
    return lax.optimization_barrier((arrays, done))[0]


def ring(array):
    node = lax.axis_size("node")
    blocks = {0: array}
    up, down = array, array
    for step in range(1, node // 2 + 1):
        up = along_node(up, -1)
        blocks[node - step] = up
        if 2 * step < node:
            down = along_node(down, 1)
            blocks[step] = down
    return [blocks[d] for d in range(node)]


def call(kernel, out, *args, scratch=(), grid=None, in_specs=None, out_specs=None, vmem=40):
    return pl.pallas_call(
        kernel,
        out_shape=out,
        in_specs=in_specs or [VMEM] * len(args),
        out_specs=out_specs or jax.tree.map(lambda _: VMEM, out),
        scratch_shapes=scratch,
        compiler_params=pltpu.CompilerParams(vmem_limit_bytes=vmem * 2**20),
        cost_estimate=pl.CostEstimate(flops=0, bytes_accessed=0, transcendentals=0),
        **({"grid": grid} if grid else {}),
    )(*args)


class Sizes:
    def __init__(self, context, grad_out, out_weight):
        self.outer, self.node = lax.axis_size("outer"), lax.axis_size("node")
        self.rows, self.cols, self.cores = plane_of(self.outer)
        self.chips = self.rows * self.cols
        self.tokens, self.held = grad_out.shape
        self.taken, self.width = out_weight.shape
        self.row = [(0, da) for da in range(1, self.cols)]
        self.column = [(db, 0) for db in range(1, self.rows)]
        self.across = [(db, da) for db in range(1, self.rows) for da in range(1, self.cols)]
        self.half, self.slabs = self.taken // 2, self.taken // self.width
        self.high = self.taken + self.slabs * self.tokens
        self.fits = self.width % 128 == 0 and self.held % (self.width * self.cores) == 0 and self.node % 2 == 0


def pack_kernel(s, weight, context, out, sems):
    moves = [(weight, 0, 0, s.half, 0)]
    moves += [(context, 0, i * s.width, s.tokens, s.half + i * s.tokens) for i in range(s.slabs)]
    moves += [(weight, s.half, 0, s.half, s.high - s.half)]
    copies = []
    for i, (source, row, column, height, to) in enumerate(moves):
        rows = source.at[pl.ds(row, height), pl.ds(column, s.width)]
        copies.append(pltpu.make_async_copy(rows, out.at[pl.ds(to, height)], sems.at[i]))
        copies[-1].start()
    for copy in copies:
        copy.wait()


def route_kernel(s, *refs):
    blocks, (mine, other, whole) = refs[: s.node], refs[s.node :]
    for d, block in enumerate(blocks):
        whole[lax.rem(lax.axis_index("node") + d, jnp.int32(s.node))] = block[...]
    for out, kind in ((mine, kind_at(0)), (other, kind_at(1))):
        for chip in range(s.chips):
            first = chip * s.cores * s.width
            at = pl.multiple_of(first % s.held + kind * s.width, 128)
            out[chip] = whole[first // s.held, :, pl.ds(at, s.width)]


def pick_kernel(s, mine, theirs, *sent):
    odd = lax.rem(lax.axis_index("node"), jnp.int32(2))
    for source, here in ((mine, odd == 0), (theirs, odd == 1)):

        @pl.when(here)
        def _(source=source):
            for (db, da), out in zip(s.across + s.row + s.column, sent):
                out[...] = source[chip_at(-db, -da)]


def put(s, packed, slot, n, share, second):
    odd = lax.rem(lax.axis_index("node"), jnp.int32(2))
    for block, half in ((share, odd), (second, 1 - odd)):
        at = pl.multiple_of((half * n + slot) * s.tokens, 128)
        packed[pl.ds(at, s.tokens)] = block[...]


def turn_kernel(s, context, *refs):
    *refs, out = refs
    n = len(s.row + s.column)
    slabs = [[pack[s.half + i * s.tokens : s.half + (i + 1) * s.tokens] for i in range(s.slabs)] for pack in refs[:n]]
    for upper, lower in zip(refs[n::2], refs[n + 1 :: 2]):
        slab = jnp.concatenate([upper[...], lower[...]], axis=0)
        slabs.append([slab[i * s.tokens : (i + 1) * s.tokens] for i in range(s.slabs)])
    out[:, : s.tokens] = context[...].T
    for k, parts in enumerate(slabs):
        to = slice((1 + k) * s.tokens, (2 + k) * s.tokens)
        for i, part in enumerate(parts):
            out[i * s.width : (i + 1) * s.width, to] = part.T


def over_chips(s, mine, theirs, pieces):
    total = 0.0
    for at, piece in pieces:
        chip = chip_at(*at)
        left = jnp.concatenate([mine[chip], theirs[chip]], axis=0)
        total += lax.dot_general(left, piece, (((1,), (1,)), ((), ())), preferred_element_type=F32)
    return total


def context_kernel(s, mine, theirs, weight, *refs):
    *packs, own, others = refs
    for h in range(2):
        side = slice(h * s.half, (h + 1) * s.half)
        pieces = [((0, 0), weight[side])]
        pieces += [(at, pack[: s.half] if h == 0 else pack[-s.half :]) for at, pack in zip(s.row + s.column, packs)]
        total = over_chips(s, mine, theirs, pieces)
        own[:, side] = total[: s.tokens]
        others[:, side] = total[s.tokens :]


def context_far_kernel(s, mine, other, near, near_theirs, *refs):
    *halves, out = refs
    quarter = len(halves) // 2
    for h in range(2):
        side = slice(h * s.half, (h + 1) * s.half)
        total = near[:, side] + near_theirs[:, side]
        for k, at in enumerate(s.across):
            for left, pairs in ((mine, halves[:quarter]), (other, halves[quarter:])):
                piece = pairs[2 * k + h][...]
                total += lax.dot_general(
                    left[chip_at(*at)], piece, (((1,), (1,)), ((), ())), preferred_element_type=F32
                )
        out[:, side] = total.astype(BF16)


def near_kernel(s, turned, theirs, mine, other, *refs):
    *blocks, out, packed = refs
    n = 1 + len(blocks) // 2
    packed[: s.tokens] = mine[chip_at(0, 0)]
    packed[n * s.tokens : (n + 1) * s.tokens] = other[chip_at(0, 0)]
    for k in range(1, n):
        put(s, packed, k, n, *blocks[2 * k - 2 : 2 * k])
    left = jnp.concatenate([turned[:, : n * s.tokens], theirs[:, : n * s.tokens]], axis=1)
    out[...] = jnp.dot(left, packed[...], preferred_element_type=F32)


def far_kernel(s, scale, near, turned, theirs, *refs):
    *blocks, out, packed = refs
    n = len(blocks) // 2
    for k in range(n):
        put(s, packed, k, n, *blocks[2 * k : 2 * k + 2])
    at = (1 + len(s.row + s.column)) * s.tokens
    left = jnp.concatenate([turned[:, at:], theirs[:, at:]], axis=1)
    out[...] = (near[...] + jnp.dot(left, packed[...], preferred_element_type=F32)) * scale


def body(context, grad_out, out_weight):
    s = Sizes(context, grad_out, out_weight)
    if not s.fits or s.cores == 1:
        return plain(context, grad_out, out_weight)
    shape = lambda *dims, dtype=BF16: jax.ShapeDtypeStruct(dims, dtype)
    scale = 1.0 / math.sqrt(s.tokens * s.outer)
    near = s.row + s.column

    around = ring(grad_out)
    pack = call(
        functools.partial(pack_kernel, s), shape(s.high, s.width), out_weight, context,
        in_specs=[pl.BlockSpec(memory_space=pl.ANY)] * 2, scratch=[pltpu.SemaphoreType.DMA((s.slabs + 2,))], vmem=60,
    )
    packs = {at: shift(pack, *at) for at in near}

    def forward(packs, first, count):
        pairs = []
        for db, da in s.across:
            pairs.append(shift(packs[0, da][first : first + count], db, 0))
            pairs.append(shift(packs[db, 0][s.high - first - count : s.high - first], 0, da))
        return pairs

    packs = after(packs, around)
    slabs = forward(packs, s.half, s.high // 2 - s.half)

    columns = shape(s.chips, s.tokens, s.width)
    mine, other = call(
        functools.partial(route_kernel, s), [columns] * 2, *around,
        scratch=[pltpu.VMEM((s.node, s.tokens, s.held), BF16)],
    )
    theirs = after(sibling(other), packs)

    chips = s.across + near
    sent = call(functools.partial(pick_kernel, s), [shape(s.tokens, s.width)] * len(chips), mine, theirs)
    shares = [shift(x, *at) for x, at in zip(sent, chips)]
    seconds = [lax.ppermute(x, "node", [(i ^ 1, i) for i in range(s.node)]) for x in shares]
    blocks = {at: two for at, two in zip(chips, zip(shares, seconds))}
    turned = call(
        functools.partial(turn_kernel, s), shape(s.taken, s.chips * s.tokens),
        *after([context, *[packs[at] for at in near], *slabs], shares),
    )
    turned_other = sibling(turned)

    packs = after(packs, shares)
    pairs = forward(packs, 0, s.half)
    packs = [packs[at] for at in near]

    def by_rows(x):
        return pl.BlockSpec((s.taken // 4, x.shape[1]), lambda i: (i, 0))

    result = shape(s.taken, s.width, dtype=F32)
    lefts = [turned, turned_other]
    rights = [mine, theirs, *[x for at in near for x in blocks[at]]]
    sums = call(
        functools.partial(near_kernel, s), result, *lefts, *rights,
        grid=(4,), in_specs=[by_rows(x) for x in lefts] + [VMEM] * len(rights), out_specs=by_rows(result),
        scratch=[pltpu.VMEM((2 * (1 + len(near)) * s.tokens, s.width), BF16)],
    )
    lefts = [sums, turned, turned_other]
    rights = [x for at in s.across for x in blocks[at]]
    weight_grad = call(
        functools.partial(far_kernel, s, scale), result, *lefts, *rights,
        grid=(4,), in_specs=[by_rows(x) for x in lefts] + [VMEM] * len(rights), out_specs=by_rows(result),
        scratch=[pltpu.VMEM((len(rights) * s.tokens, s.width), BF16)],
    )

    half_sums = shape(s.tokens, s.taken, dtype=F32)
    own, others = call(functools.partial(context_kernel, s), [half_sums] * 2, mine, theirs, out_weight, *after(packs, turned_other))
    pairs_other = [sibling(x) for x in after(pairs, (sums, seconds))]
    context_grad = call(
        functools.partial(context_far_kernel, s), shape(s.tokens, s.taken),
        mine, other, own, sibling(others), *pairs, *pairs_other,
    )
    return (context_grad, weight_grad)


def plain(context, grad_out, out_weight):
    grad_full = lax.all_gather(grad_out, "node", axis=1, tiled=True)
    weight = lax.all_gather(out_weight, "outer", axis=1, tiled=True)
    context_grad = lax.dot_general(grad_full, weight, (((1,), (1,)), ((), ())), preferred_element_type=F32)
    scale = 1.0 / math.sqrt(grad_full.shape[0] * lax.axis_size("outer"))
    owner_cols = lax.all_to_all(grad_full, "outer", split_axis=1, concat_axis=0, tiled=True)
    context = lax.all_gather(context, "outer", axis=0, tiled=True)
    weight_grad = lax.dot_general(context, owner_cols, (((0,), (0,)), ((), ())), preferred_element_type=F32)
    return (context_grad.astype(BF16), weight_grad * scale)


def solution(mesh):
    in_specs = (P("outer", "node"), P("outer", "node"), P("node", "outer"))
    out_specs = (P("outer", "node"), P("node", "outer"))
    return jax.shard_map(body, mesh=mesh, in_specs=in_specs, out_specs=out_specs, check_vma=False)
```

```python
import functools
import math

import jax
import jax.numpy as jnp
from jax import lax
from jax.experimental import pallas as pl
from jax.experimental.pallas import tpu as pltpu
from jax.sharding import PartitionSpec as P

F32, BF16 = jnp.float32, jnp.bfloat16
VMEM = pl.BlockSpec(memory_space=pltpu.VMEM)


def plane_of(outer):
    cores = 2 if outer % 2 == 0 else 1
    chips = outer // cores
    cols = max(d for d in range(1, math.isqrt(chips) + 1) if chips % d == 0)
    return chips // cols, cols, cores


def place(o, db, da, dc):
    rows, cols, cores = plane_of(lax.axis_size("outer"))
    b, a, c = o // (cols * cores), o // cores % cols, o % cores
    return ((b + db) % rows * cols + (a + da) % cols) * cores + (c + dc) % cores


def chip_at(db, da):
    rows, cols, cores = plane_of(lax.axis_size("outer"))
    chip = lax.div(lax.axis_index("outer"), jnp.int32(cores))
    b, a = lax.div(chip, jnp.int32(cols)), lax.rem(chip, jnp.int32(cols))
    return lax.rem(b + db % rows, jnp.int32(rows)) * cols + lax.rem(a + da % cols, jnp.int32(cols))


def kind_at(dc):
    cores = plane_of(lax.axis_size("outer"))[2]
    return lax.rem(lax.axis_index("outer") + dc, jnp.int32(cores))


def shift(array, db, da, dc=0):
    return lax.ppermute(array, "outer", [(place(o, db, da, dc), o) for o in range(lax.axis_size("outer"))])


def sibling(array, cuts=()):
    at = [0] + [int(array.shape[0] * cut) for cut in cuts] + [array.shape[0]]
    pieces = [shift(array[i:j], 0, 0, 1) for i, j in zip(at, at[1:])]
    return pieces[0] if len(pieces) == 1 else jnp.concatenate(pieces)


def along_node(array, d):
    node = lax.axis_size("node")
    return lax.ppermute(array, "node", [((i + d) % node, i) for i in range(node)])


def after(arrays, done):
    return lax.optimization_barrier((arrays, done))[0]


def call(kernel, out, *args, scratch=(), grid=None, in_specs=None, out_specs=None, vmem=40):
    return pl.pallas_call(
        kernel,
        out_shape=out,
        in_specs=in_specs or [VMEM] * len(args),
        out_specs=out_specs or jax.tree.map(lambda _: VMEM, out),
        scratch_shapes=scratch,
        compiler_params=pltpu.CompilerParams(vmem_limit_bytes=vmem * 2**20),
        cost_estimate=pl.CostEstimate(flops=0, bytes_accessed=0, transcendentals=0),
        **({"grid": grid} if grid else {}),
    )(*args)


class Sizes:
    def __init__(self, context, grad_out, out_weight):
        self.outer, self.node = lax.axis_size("outer"), lax.axis_size("node")
        self.rows, self.cols, self.cores = plane_of(self.outer)
        self.chips = self.rows * self.cols
        self.tokens, self.held = grad_out.shape
        self.taken, self.width = out_weight.shape
        self.row = [(0, da) for da in range(1, self.cols)]
        self.column = [(db, 0) for db in range(1, self.rows)]
        self.across = [(db, da) for db in range(1, self.rows) for da in range(1, self.cols)]
        self.half = self.taken // 2
        self.fits = self.width % 128 == 0 and self.held % (self.width * self.cores) == 0 and self.node % 2 == 0 and self.node > 2


def route_kernel(s, *refs):
    blocks, (mine, other, whole) = refs[: s.node], refs[s.node :]
    for d, block in enumerate(blocks):
        whole[lax.rem(lax.axis_index("node") + d, jnp.int32(s.node))] = block[...]
    for out, kind in ((mine, kind_at(0)), (other, kind_at(1))):
        for chip in range(s.chips):
            first = chip * s.cores * s.width
            at = pl.multiple_of(first % s.held + kind * s.width, 128)
            out[chip] = whole[first // s.held, :, pl.ds(at, s.width)]


def pick_kernel(s, mine, theirs, *sent):
    odd = lax.rem(lax.axis_index("node"), jnp.int32(2))
    for (db, da), out in zip(s.row + s.column, sent):
        out[: s.tokens] = mine[chip_at(-db, -da)]
        out[s.tokens :] = theirs[chip_at(-db, -da)]
    for source, here in ((mine, odd == 0), (theirs, odd == 1)):

        @pl.when(here)
        def _(source=source):
            for (db, da), out in zip(s.across, sent[len(s.row + s.column) :]):
                out[...] = source[chip_at(-db, -da)]


def put(s, packed, slot, n, share, second):
    odd = lax.rem(lax.axis_index("node"), jnp.int32(2))
    for block, half in ((share, odd), (second, 1 - odd)):
        at = pl.multiple_of((half * n + slot) * s.tokens, 128)
        packed[pl.ds(at, s.tokens)] = block[...]


def turn_kernel(s, *refs):
    *blocks, out = refs
    at = 0
    for block in blocks:
        out[:, at : at + block.shape[0]] = block[...].T
        at += block.shape[0]


def over_chips(s, mine, theirs, pieces):
    total = 0.0
    for at, piece in pieces:
        chip = chip_at(*at)
        left = jnp.concatenate([mine[chip], theirs[chip]], axis=0)
        total += lax.dot_general(left, piece, (((1,), (1,)), ((), ())), preferred_element_type=F32)
    return total


def context_kernel(s, mine, theirs, *refs):
    *weights, out = refs
    for h in range(2):
        side = slice(h * s.half, (h + 1) * s.half)
        pieces = [(at, weight[side]) for at, weight in zip([(0, 0)] + s.row + s.column, weights)]
        out[:, side] = over_chips(s, mine, theirs, pieces)


def context_far_kernel(s, mine, theirs, near, *refs):
    *pairs, own, others = refs
    for h in range(2):
        side = slice(h * s.half, (h + 1) * s.half)
        total = near[:, side] + over_chips(s, mine, theirs, [(at, pairs[2 * k + h][...]) for k, at in enumerate(s.across)])
        own[:, side] = total[: s.tokens]
        others[:, side] = total[s.tokens :]


def early_kernel(s, turned, theirs, far, far_theirs, mine, other, *refs):
    *blocks, out, packed = refs
    n = 1 + len(blocks) // 2
    packed[: s.tokens] = mine[chip_at(0, 0)]
    packed[n * s.tokens : (n + 1) * s.tokens] = other[chip_at(0, 0)]
    for k in range(1, n):
        put(s, packed, k, n, *blocks[2 * k - 2 : 2 * k])
    left = [turned[:, : s.tokens], far[...], theirs[:, : s.tokens], far_theirs[...]]
    out[...] = jnp.dot(jnp.concatenate(left, axis=1), packed[...], preferred_element_type=F32)


def late_kernel(s, scale, early, turned, theirs, *refs):
    *blocks, out, packed = refs
    n = len(blocks)
    for k, block in enumerate(blocks):
        packed[k * s.tokens : (k + 1) * s.tokens] = block[: s.tokens]
        packed[(n + k) * s.tokens : (n + k + 1) * s.tokens] = block[s.tokens :]
    left = jnp.concatenate([turned[:, s.tokens :], theirs[:, s.tokens :]], axis=1)
    out[...] = (early[...] + jnp.dot(left, packed[...], preferred_element_type=F32)) * scale


def body(context, grad_out, out_weight):
    s = Sizes(context, grad_out, out_weight)
    if not s.fits or s.cores == 1:
        return plain(context, grad_out, out_weight)
    shape = lambda *dims, dtype=BF16: jax.ShapeDtypeStruct(dims, dtype)
    scale = 1.0 / math.sqrt(s.tokens * s.outer)
    near = s.row + s.column

    def straight(block):
        return {at: shift(block, *at) for at in near}

    def diagonal(blocks):
        half = next(iter(blocks.values())).shape[0] // 2
        pairs = []
        for db, da in s.across:
            pairs.append(shift(blocks[0, da][:half], db, 0))
            pairs.append(shift(blocks[db, 0][half:], 0, da))
        return pairs

    weights = straight(out_weight)
    around = {0: grad_out, s.node - 1: along_node(grad_out, -1), 1: along_node(grad_out, 1)}
    contexts = {at: shift(context, *at) for at in s.row}
    contexts |= {at: shift(after(context, around[s.node - 1]), *at) for at in s.column}
    weights, around = lax.optimization_barrier((weights, around))
    for step in range(2, s.node // 2 + 1):
        around[s.node - step] = along_node(around[s.node - step + 1], -1)
        if 2 * step < s.node:
            around[step] = along_node(around[step - 1], 1)
    weights_far = diagonal(weights)
    contexts_far = diagonal(contexts)
    turn = functools.partial(turn_kernel, s)
    turned = call(turn, shape(s.taken, (1 + len(near)) * s.tokens), context, *contexts.values())
    turned_other = sibling(turned)
    turned_far = call(turn, shape(s.taken, len(s.across) * s.tokens), *contexts_far)
    turned_far_other = sibling(turned_far, ())

    columns = shape(s.chips, s.tokens, s.width)
    mine, other = call(
        functools.partial(route_kernel, s), [columns] * 2, *[around[d] for d in range(s.node)],
        scratch=[pltpu.VMEM((s.node, s.tokens, s.held), BF16)],
    )
    theirs = sibling(after(other, weights_far))

    outs = [shape(s.cores * s.tokens, s.width)] * len(near) + [shape(s.tokens, s.width)] * len(s.across)
    sent = call(functools.partial(pick_kernel, s), outs, mine, after(theirs, turned_other))
    shares = [shift(x, *at) for x, at in zip(sent[len(near) :], s.across)]
    blocks = [shift(x, *at) for x, at in zip(sent, near)]
    far = [(x, lax.ppermute(x, "node", [(i ^ 1, i) for i in range(s.node)])) for x in shares]

    half_sums = shape(s.tokens, s.taken, dtype=F32)
    sums = call(
        functools.partial(context_kernel, s), shape(s.cores * s.tokens, s.taken, dtype=F32),
        mine, theirs, out_weight, *weights.values(),
    )
    own, others = call(functools.partial(context_far_kernel, s), [half_sums] * 2, mine, theirs, sums, *weights_far)
    context_grad = (own + sibling(others, (0.25, 0.5, 0.75))).astype(BF16)

    def by_rows(x):
        return pl.BlockSpec((s.taken // 4, x.shape[1]), lambda i: (i, 0))

    result = shape(s.taken, s.width, dtype=F32)
    lefts = [turned, turned_other, turned_far, turned_far_other]
    rights = [mine, theirs, *[x for two in far for x in two]]
    early = call(
        functools.partial(early_kernel, s), result, *lefts, *rights,
        grid=(4,), in_specs=[by_rows(x) for x in lefts] + [VMEM] * len(rights), out_specs=by_rows(result),
        scratch=[pltpu.VMEM((2 * (1 + len(far)) * s.tokens, s.width), BF16)],
    )
    lefts = [early, turned, turned_other]
    weight_grad = call(
        functools.partial(late_kernel, s, scale), result, *lefts, *blocks,
        grid=(4,), in_specs=[by_rows(x) for x in lefts] + [VMEM] * len(blocks), out_specs=by_rows(result),
        scratch=[pltpu.VMEM((2 * len(blocks) * s.tokens, s.width), BF16)],
    )
    return (context_grad, weight_grad)


def plain(context, grad_out, out_weight):
    grad_full = lax.all_gather(grad_out, "node", axis=1, tiled=True)
    weight = lax.all_gather(out_weight, "outer", axis=1, tiled=True)
    context_grad = lax.dot_general(grad_full, weight, (((1,), (1,)), ((), ())), preferred_element_type=F32)
    scale = 1.0 / math.sqrt(grad_full.shape[0] * lax.axis_size("outer"))
    owner_cols = lax.all_to_all(grad_full, "outer", split_axis=1, concat_axis=0, tiled=True)
    context = lax.all_gather(context, "outer", axis=0, tiled=True)
    weight_grad = lax.dot_general(context, owner_cols, (((0,), (0,)), ((), ())), preferred_element_type=F32)
    return (context_grad.astype(BF16), weight_grad * scale)


def solution(mesh):
    in_specs = (P("outer", "node"), P("outer", "node"), P("node", "outer"))
    out_specs = (P("outer", "node"), P("node", "outer"))
    return jax.shard_map(body, mesh=mesh, in_specs=in_specs, out_specs=out_specs, check_vma=False)
```

```python
import functools
import math

import jax
import jax.numpy as jnp
from jax import lax
from jax.experimental import pallas as pl
from jax.experimental.pallas import tpu as pltpu
from jax.sharding import PartitionSpec as P

F32, BF16 = jnp.float32, jnp.bfloat16
VMEM = pl.BlockSpec(memory_space=pltpu.VMEM)


def plane_of(outer):
    cores = 2 if outer % 2 == 0 else 1
    chips = outer // cores
    cols = max(d for d in range(1, math.isqrt(chips) + 1) if chips % d == 0)
    return chips // cols, cols, cores


def place(o, db, da, dc):
    rows, cols, cores = plane_of(lax.axis_size("outer"))
    b, a, c = o // (cols * cores), o // cores % cols, o % cores
    return ((b + db) % rows * cols + (a + da) % cols) * cores + (c + dc) % cores


def chip_at(db, da):
    rows, cols, cores = plane_of(lax.axis_size("outer"))
    chip = lax.div(lax.axis_index("outer"), jnp.int32(cores))
    b, a = lax.div(chip, jnp.int32(cols)), lax.rem(chip, jnp.int32(cols))
    return lax.rem(b + db % rows, jnp.int32(rows)) * cols + lax.rem(a + da % cols, jnp.int32(cols))


def kind_at(dc):
    cores = plane_of(lax.axis_size("outer"))[2]
    return lax.rem(lax.axis_index("outer") + dc, jnp.int32(cores))


def shift(array, db, da, dc=0):
    return lax.ppermute(array, "outer", [(place(o, db, da, dc), o) for o in range(lax.axis_size("outer"))])


def sibling(array, cuts=()):
    at = [0] + [int(array.shape[0] * cut) for cut in cuts] + [array.shape[0]]
    pieces = [shift(array[i:j], 0, 0, 1) for i, j in zip(at, at[1:])]
    return pieces[0] if len(pieces) == 1 else jnp.concatenate(pieces)


def along_node(array, d):
    node = lax.axis_size("node")
    return lax.ppermute(array, "node", [((i + d) % node, i) for i in range(node)])


def after(arrays, done):
    return lax.optimization_barrier((arrays, done))[0]


def call(kernel, out, *args, scratch=(), out_specs=None):
    return pl.pallas_call(
        kernel,
        out_shape=out,
        in_specs=[VMEM] * len(args),
        out_specs=out_specs or jax.tree.map(lambda _: VMEM, out),
        scratch_shapes=scratch,
        compiler_params=pltpu.CompilerParams(vmem_limit_bytes=40 * 2**20),
        cost_estimate=pl.CostEstimate(flops=0, bytes_accessed=0, transcendentals=0),
    )(*args)


class Sizes:
    def __init__(self, context, grad_out, out_weight):
        self.outer, self.node = lax.axis_size("outer"), lax.axis_size("node")
        self.rows, self.cols, self.cores = plane_of(self.outer)
        self.chips = self.rows * self.cols
        self.tokens, self.held = grad_out.shape
        self.taken, self.width = out_weight.shape
        self.row = [(0, da) for da in range(1, self.cols)]
        self.column = [(db, 0) for db in range(1, self.rows)]
        self.across = [(db, da) for db in range(1, self.rows) for da in range(1, self.cols)]
        self.half = self.taken // 2
        self.fits = self.width % 128 == 0 and self.held % (self.width * self.cores) == 0 and self.node % 2 == 0 and self.node > 2


def route_kernel(s, *refs):
    blocks, (mine, other, whole) = refs[: s.node], refs[s.node :]
    for d, block in enumerate(blocks):
        whole[lax.rem(lax.axis_index("node") + d, jnp.int32(s.node))] = block[...]
    for out, kind in ((mine, kind_at(0)), (other, kind_at(1))):
        for chip in range(s.chips):
            first = chip * s.cores * s.width
            at = pl.multiple_of(first % s.held + kind * s.width, 128)
            out[chip] = whole[first // s.held, :, pl.ds(at, s.width)]


def pick_kernel(s, mine, theirs, *sent):
    odd = lax.rem(lax.axis_index("node"), jnp.int32(2))
    for (db, da), out in zip(s.row + s.column, sent):
        out[: s.tokens] = mine[chip_at(-db, -da)]
        out[s.tokens :] = theirs[chip_at(-db, -da)]
    for source, here in ((mine, odd == 0), (theirs, odd == 1)):

        @pl.when(here)
        def _(source=source):
            for (db, da), out in zip(s.across, sent[len(s.row + s.column) :]):
                out[...] = source[chip_at(-db, -da)]


def put(s, packed, slot, n, share, second):
    odd = lax.rem(lax.axis_index("node"), jnp.int32(2))
    for block, half in ((share, odd), (second, 1 - odd)):
        at = pl.multiple_of((half * n + slot) * s.tokens, 128)
        packed[pl.ds(at, s.tokens)] = block[...]


def turn_kernel(s, *refs):
    *blocks, out = refs
    at = 0
    for block in blocks:
        out[:, at : at + block.shape[0]] = block[...].T
        at += block.shape[0]


def over_chips(s, mine, theirs, pieces):
    total = 0.0
    for at, piece in pieces:
        chip = chip_at(*at)
        left = jnp.concatenate([mine[chip], theirs[chip]], axis=0)
        total += lax.dot_general(left, piece, (((1,), (1,)), ((), ())), preferred_element_type=F32)
    return total


def context_kernel(s, mine, theirs, *refs):
    *weights, out = refs
    for h in range(2):
        side = slice(h * s.half, (h + 1) * s.half)
        pieces = [(at, weight[side]) for at, weight in zip([(0, 0)] + s.row + s.column, weights)]
        out[:, side] = over_chips(s, mine, theirs, pieces)


def context_far_kernel(s, mine, theirs, near, *refs):
    *pairs, own, others = refs
    for h in range(2):
        side = slice(h * s.half, (h + 1) * s.half)
        total = near[:, side] + over_chips(s, mine, theirs, [(at, pairs[2 * k + h][...]) for k, at in enumerate(s.across)])
        own[:, side] = total[: s.tokens]
        others[:, side] = total[s.tokens :]


def blocks_of(rows):
    return [slice(i * rows // 4, (i + 1) * rows // 4) for i in range(4)]


def early_kernel(s, turned, theirs, far, far_theirs, mine, other, *refs):
    *blocks, out, packed = refs
    n = 1 + len(blocks) // 2
    packed[: s.tokens] = mine[chip_at(0, 0)]
    packed[n * s.tokens : (n + 1) * s.tokens] = other[chip_at(0, 0)]
    for k in range(1, n):
        put(s, packed, k, n, *blocks[2 * k - 2 : 2 * k])
    for rows in blocks_of(s.taken):
        left = [turned[rows, : s.tokens], far[rows], theirs[rows, : s.tokens], far_theirs[rows]]
        out[rows] = jnp.dot(jnp.concatenate(left, axis=1), packed[...], preferred_element_type=F32)


def late_kernel(s, scale, early, turned, theirs, *refs):
    *blocks, out, packed, sums, sems = refs
    n = len(blocks)
    for k, block in enumerate(blocks):
        packed[k * s.tokens : (k + 1) * s.tokens] = block[: s.tokens]
        packed[(n + k) * s.tokens : (n + k + 1) * s.tokens] = block[s.tokens :]
    copies = []
    for i, rows in enumerate(blocks_of(s.taken)):
        left = jnp.concatenate([turned[rows, s.tokens :], theirs[rows, s.tokens :]], axis=1)
        sums[rows] = (early[rows] + jnp.dot(left, packed[...], preferred_element_type=F32)) * scale
        copies.append(pltpu.make_async_copy(sums.at[rows], out.at[rows], sems.at[i]))
        copies[-1].start()
    for copy in copies:
        copy.wait()


def body(context, grad_out, out_weight):
    s = Sizes(context, grad_out, out_weight)
    if not s.fits or s.cores == 1:
        return plain(context, grad_out, out_weight)
    shape = lambda *dims, dtype=BF16: jax.ShapeDtypeStruct(dims, dtype)
    scale = 1.0 / math.sqrt(s.tokens * s.outer)
    near = s.row + s.column

    def straight(block):
        return {at: shift(block, *at) for at in near}

    def diagonal(blocks):
        half = next(iter(blocks.values())).shape[0] // 2
        pairs = []
        for db, da in s.across:
            pairs.append(shift(blocks[0, da][:half], db, 0))
            pairs.append(shift(blocks[db, 0][half:], 0, da))
        return pairs

    weights = straight(out_weight)
    around = {0: grad_out, s.node - 1: along_node(grad_out, -1), 1: along_node(grad_out, 1)}
    contexts = {at: shift(context, *at) for at in s.row}
    contexts |= {at: shift(after(context, around[s.node - 1]), *at) for at in s.column}
    weights, around = lax.optimization_barrier((weights, around))
    for step in range(2, s.node // 2 + 1):
        around[s.node - step] = along_node(around[s.node - step + 1], -1)
        if 2 * step < s.node:
            around[step] = along_node(around[step - 1], 1)
    weights_far = diagonal(weights)
    contexts_far = diagonal(contexts)
    turn = functools.partial(turn_kernel, s)
    turned = call(turn, shape(s.taken, (1 + len(near)) * s.tokens), context, *contexts.values())
    turned_other = sibling(turned)
    turned_far = call(turn, shape(s.taken, len(s.across) * s.tokens), *contexts_far)
    turned_far_other = sibling(turned_far, ())

    columns = shape(s.chips, s.tokens, s.width)
    mine, other = call(
        functools.partial(route_kernel, s), [columns] * 2, *[around[d] for d in range(s.node)],
        scratch=[pltpu.VMEM((s.node, s.tokens, s.held), BF16)],
    )
    theirs = sibling(after(other, weights_far))

    outs = [shape(s.cores * s.tokens, s.width)] * len(near) + [shape(s.tokens, s.width)] * len(s.across)
    sent = call(functools.partial(pick_kernel, s), outs, mine, after(theirs, turned_other))
    shares = [shift(x, *at) for x, at in zip(sent[len(near) :], s.across)]
    blocks = [shift(x, *at) for x, at in zip(sent, near)]
    far = [(x, lax.ppermute(x, "node", [(i ^ 1, i) for i in range(s.node)])) for x in shares]

    half_sums = shape(s.tokens, s.taken, dtype=F32)
    sums = call(
        functools.partial(context_kernel, s), shape(s.cores * s.tokens, s.taken, dtype=F32),
        mine, theirs, out_weight, *weights.values(),
    )
    own, others = call(functools.partial(context_far_kernel, s), [half_sums] * 2, mine, theirs, sums, *weights_far)
    context_grad = (own + sibling(others, (0.25, 0.5, 0.75))).astype(BF16)

    result = shape(s.taken, s.width, dtype=F32)
    early = call(
        functools.partial(early_kernel, s), result,
        turned, turned_other, turned_far, turned_far_other, mine, theirs, *[x for two in far for x in two],
        scratch=[pltpu.VMEM((2 * (1 + len(far)) * s.tokens, s.width), BF16)],
    )
    weight_grad = call(
        functools.partial(late_kernel, s, scale), result, early, turned, turned_other, *blocks,
        out_specs=pl.BlockSpec(memory_space=pl.ANY),
        scratch=[
            pltpu.VMEM((2 * len(blocks) * s.tokens, s.width), BF16),
            pltpu.VMEM((s.taken, s.width), F32),
            pltpu.SemaphoreType.DMA((4,)),
        ],
    )
    return (context_grad, weight_grad)


def plain(context, grad_out, out_weight):
    grad_full = lax.all_gather(grad_out, "node", axis=1, tiled=True)
    weight = lax.all_gather(out_weight, "outer", axis=1, tiled=True)
    context_grad = lax.dot_general(grad_full, weight, (((1,), (1,)), ((), ())), preferred_element_type=F32)
    scale = 1.0 / math.sqrt(grad_full.shape[0] * lax.axis_size("outer"))
    owner_cols = lax.all_to_all(grad_full, "outer", split_axis=1, concat_axis=0, tiled=True)
    context = lax.all_gather(context, "outer", axis=0, tiled=True)
    weight_grad = lax.dot_general(context, owner_cols, (((0,), (0,)), ((), ())), preferred_element_type=F32)
    return (context_grad.astype(BF16), weight_grad * scale)


def solution(mesh):
    in_specs = (P("outer", "node"), P("outer", "node"), P("node", "outer"))
    out_specs = (P("outer", "node"), P("node", "outer"))
    return jax.shard_map(body, mesh=mesh, in_specs=in_specs, out_specs=out_specs, check_vma=False)
```

```python
import functools
import math

import jax
import jax.numpy as jnp
from jax import lax
from jax.experimental import pallas as pl
from jax.experimental.pallas import tpu as pltpu
from jax.sharding import PartitionSpec as P

F32, BF16 = jnp.float32, jnp.bfloat16
VMEM = pl.BlockSpec(memory_space=pltpu.VMEM)


def plane_of(outer):
    cores = 2 if outer % 2 == 0 else 1
    chips = outer // cores
    cols = max(d for d in range(1, math.isqrt(chips) + 1) if chips % d == 0)
    return chips // cols, cols, cores


def place(o, db, da, dc):
    rows, cols, cores = plane_of(lax.axis_size("outer"))
    b, a, c = o // (cols * cores), o // cores % cols, o % cores
    return ((b + db) % rows * cols + (a + da) % cols) * cores + (c + dc) % cores


def chip_at(db, da):
    rows, cols, cores = plane_of(lax.axis_size("outer"))
    chip = lax.div(lax.axis_index("outer"), jnp.int32(cores))
    b, a = lax.div(chip, jnp.int32(cols)), lax.rem(chip, jnp.int32(cols))
    return lax.rem(b + db % rows, jnp.int32(rows)) * cols + lax.rem(a + da % cols, jnp.int32(cols))


def kind_at(dc):
    cores = plane_of(lax.axis_size("outer"))[2]
    return lax.rem(lax.axis_index("outer") + dc, jnp.int32(cores))


def shift(array, db, da, dc=0):
    return lax.ppermute(array, "outer", [(place(o, db, da, dc), o) for o in range(lax.axis_size("outer"))])


def sibling(array, cuts=()):
    at = [0] + [int(array.shape[0] * cut) for cut in cuts] + [array.shape[0]]
    pieces = [shift(array[i:j], 0, 0, 1) for i, j in zip(at, at[1:])]
    return pieces[0] if len(pieces) == 1 else jnp.concatenate(pieces)


def along_node(array, d):
    node = lax.axis_size("node")
    return lax.ppermute(array, "node", [((i + d) % node, i) for i in range(node)])


def after(arrays, done):
    return lax.optimization_barrier((arrays, done))[0]


def call(kernel, out, *args, scratch=(), out_specs=None):
    return pl.pallas_call(
        kernel,
        out_shape=out,
        in_specs=[VMEM] * len(args),
        out_specs=out_specs or jax.tree.map(lambda _: VMEM, out),
        scratch_shapes=scratch,
        compiler_params=pltpu.CompilerParams(vmem_limit_bytes=40 * 2**20),
    )(*args)


class Sizes:
    def __init__(self, context, grad_out, out_weight):
        self.outer, self.node = lax.axis_size("outer"), lax.axis_size("node")
        self.rows, self.cols, self.cores = plane_of(self.outer)
        self.chips = self.rows * self.cols
        self.tokens, self.held = grad_out.shape
        self.taken, self.width = out_weight.shape
        self.row = [(0, da) for da in range(1, self.cols)]
        self.column = [(db, 0) for db in range(1, self.rows)]
        self.across = [(db, da) for db in range(1, self.rows) for da in range(1, self.cols)]
        self.half = self.taken // 2
        whole = self.held % (self.width * self.cores) == 0 and self.node % 2 == 0 and self.node > 2
        self.fits = whole and self.width % 128 == 0 and self.tokens % 128 == 0 and self.taken % 256 == 0


def route_kernel(s, *refs):
    blocks, (mine, other, whole) = refs[: s.node], refs[s.node :]
    for d, block in enumerate(blocks):
        whole[lax.rem(lax.axis_index("node") + d, jnp.int32(s.node))] = block[...]
    for out, kind in ((mine, kind_at(0)), (other, kind_at(1))):
        for chip in range(s.chips):
            first = chip * s.cores * s.width
            at = pl.multiple_of(first % s.held + kind * s.width, 128)
            out[chip] = whole[first // s.held, :, pl.ds(at, s.width)]


def pick_kernel(s, mine, theirs, *sent):
    odd = lax.rem(lax.axis_index("node"), jnp.int32(2))
    for (db, da), out in zip(s.row + s.column, sent):
        out[: s.tokens] = mine[chip_at(-db, -da)]
        out[s.tokens :] = theirs[chip_at(-db, -da)]
    for source, here in ((mine, odd == 0), (theirs, odd == 1)):

        @pl.when(here)
        def _(source=source):
            for (db, da), out in zip(s.across, sent[len(s.row + s.column) :]):
                out[...] = source[chip_at(-db, -da)]


def put(s, packed, slot, n, share, second):
    odd = lax.rem(lax.axis_index("node"), jnp.int32(2))
    for block, half in ((share, odd), (second, 1 - odd)):
        at = pl.multiple_of((half * n + slot) * s.tokens, 128)
        packed[pl.ds(at, s.tokens)] = block[...]


def turn_kernel(s, *refs):
    *blocks, out = refs
    at = 0
    for block in blocks:
        out[:, at : at + block.shape[0]] = block[...].T
        at += block.shape[0]


def over_chips(s, mine, theirs, pieces):
    total = 0.0
    for at, piece in pieces:
        chip = chip_at(*at)
        left = jnp.concatenate([mine[chip], theirs[chip]], axis=0)
        total += lax.dot_general(left, piece, (((1,), (1,)), ((), ())), preferred_element_type=F32)
    return total


def context_kernel(s, mine, theirs, *refs):
    *weights, out = refs
    for h in range(2):
        side = slice(h * s.half, (h + 1) * s.half)
        pieces = [(at, weight[side]) for at, weight in zip([(0, 0)] + s.row + s.column, weights)]
        out[:, side] = over_chips(s, mine, theirs, pieces)


def context_far_kernel(s, mine, theirs, near, *refs):
    *pairs, own, others = refs
    for h in range(2):
        side = slice(h * s.half, (h + 1) * s.half)
        total = near[:, side] + over_chips(s, mine, theirs, [(at, pairs[2 * k + h][...]) for k, at in enumerate(s.across)])
        own[:, side] = total[: s.tokens]
        others[:, side] = total[s.tokens :]


def blocks_of(rows):
    return [slice(i * rows // 4, (i + 1) * rows // 4) for i in range(4)]


def early_kernel(s, turned, theirs, far, far_theirs, mine, other, *refs):
    *blocks, out, packed = refs
    n = 1 + len(blocks) // 2
    packed[: s.tokens] = mine[chip_at(0, 0)]
    packed[n * s.tokens : (n + 1) * s.tokens] = other[chip_at(0, 0)]
    for k in range(1, n):
        put(s, packed, k, n, *blocks[2 * k - 2 : 2 * k])
    for rows in blocks_of(s.taken):
        left = [turned[rows, : s.tokens], far[rows], theirs[rows, : s.tokens], far_theirs[rows]]
        out[rows] = jnp.dot(jnp.concatenate(left, axis=1), packed[...], preferred_element_type=F32)


def add_kernel(s, k, sums, turned, theirs, block, out):
    at = slice((1 + k) * s.tokens, (2 + k) * s.tokens)
    for rows in blocks_of(s.taken):
        left = jnp.concatenate([turned[rows, at], theirs[rows, at]], axis=1)
        out[rows] = sums[rows] + jnp.dot(left, block[...], preferred_element_type=F32)


def last_kernel(s, scale, k, sums, turned, theirs, block, out, done, sems):
    at = slice((1 + k) * s.tokens, (2 + k) * s.tokens)
    copies = []
    for i, rows in enumerate(blocks_of(s.taken)):
        left = jnp.concatenate([turned[rows, at], theirs[rows, at]], axis=1)
        done[rows] = (sums[rows] + jnp.dot(left, block[...], preferred_element_type=F32)) * scale
        copies.append(pltpu.make_async_copy(done.at[rows], out.at[rows], sems.at[i]))
        copies[-1].start()
    for copy in copies:
        copy.wait()


def body(context, grad_out, out_weight):
    s = Sizes(context, grad_out, out_weight)
    if not s.fits or s.cores == 1:
        return plain(context, grad_out, out_weight)
    shape = lambda *dims, dtype=BF16: jax.ShapeDtypeStruct(dims, dtype)
    scale = 1.0 / math.sqrt(s.tokens * s.outer)
    near = s.row + s.column

    def straight(block):
        return {at: shift(block, *at) for at in near}

    def diagonal(blocks):
        half = next(iter(blocks.values())).shape[0] // 2
        pairs = []
        for db, da in s.across:
            pairs.append(shift(blocks[0, da][:half], db, 0))
            pairs.append(shift(blocks[db, 0][half:], 0, da))
        return pairs

    weights = straight(out_weight)
    around = {0: grad_out, s.node - 1: along_node(grad_out, -1), 1: along_node(grad_out, 1)}
    contexts = {at: shift(context, *at) for at in s.row}
    contexts |= {at: shift(after(context, around[s.node - 1]), *at) for at in s.column}
    weights, around = lax.optimization_barrier((weights, around))
    for step in range(2, s.node // 2 + 1):
        around[s.node - step] = along_node(around[s.node - step + 1], -1)
        if 2 * step < s.node:
            around[step] = along_node(around[step - 1], 1)
    weights_far = diagonal(weights)
    contexts_far = diagonal(contexts)
    turn = functools.partial(turn_kernel, s)
    turned = call(turn, shape(s.taken, (1 + len(near)) * s.tokens), context, *contexts.values())
    turned_other = sibling(turned)
    turned_far = call(turn, shape(s.taken, len(s.across) * s.tokens), *contexts_far)
    turned_far_other = sibling(turned_far)

    columns = shape(s.chips, s.tokens, s.width)
    mine, other = call(
        functools.partial(route_kernel, s), [columns] * 2, *[around[d] for d in range(s.node)],
        scratch=[pltpu.VMEM((s.node, s.tokens, s.held), BF16)],
    )
    theirs = sibling(after(other, weights_far))

    outs = [shape(s.cores * s.tokens, s.width)] * len(near) + [shape(s.tokens, s.width)] * len(s.across)
    sent = call(functools.partial(pick_kernel, s), outs, mine, after(theirs, turned_other))
    shares = [shift(x, *at) for x, at in zip(sent[len(near) :], s.across)]
    blocks = [shift(x, *at) for x, at in zip(sent, near)]
    far = [(x, lax.ppermute(x, "node", [(i ^ 1, i) for i in range(s.node)])) for x in shares]

    half_sums = shape(s.tokens, s.taken, dtype=F32)
    near_sums = call(
        functools.partial(context_kernel, s), shape(s.cores * s.tokens, s.taken, dtype=F32),
        mine, theirs, out_weight, *after([*weights.values()], turned_other),
    )
    own, others = call(functools.partial(context_far_kernel, s), [half_sums] * 2, mine, theirs, near_sums, *weights_far)
    context_grad = (own + sibling(others, (0.4375, 0.875))).astype(BF16)

    result = shape(s.taken, s.width, dtype=F32)
    sums = call(
        functools.partial(early_kernel, s), result,
        turned, turned_other, turned_far, turned_far_other, mine, theirs, *[x for two in far for x in two],
        scratch=[pltpu.VMEM((2 * (1 + len(far)) * s.tokens, s.width), BF16)],
    )
    for k, block in enumerate(blocks[:-1]):
        sums = call(functools.partial(add_kernel, s, k), result, sums, turned, turned_other, block)
    weight_grad = call(
        functools.partial(last_kernel, s, scale, len(blocks) - 1), result, sums, turned, turned_other, blocks[-1],
        out_specs=pl.BlockSpec(memory_space=pl.ANY),
        scratch=[pltpu.VMEM((s.taken, s.width), F32), pltpu.SemaphoreType.DMA((4,))],
    )
    return (context_grad, weight_grad)


def plain(context, grad_out, out_weight):
    grad_full = lax.all_gather(grad_out, "node", axis=1, tiled=True)
    weight = lax.all_gather(out_weight, "outer", axis=1, tiled=True)
    context_grad = lax.dot_general(grad_full, weight, (((1,), (1,)), ((), ())), preferred_element_type=F32)
    scale = 1.0 / math.sqrt(grad_full.shape[0] * lax.axis_size("outer"))
    owner_cols = lax.all_to_all(grad_full, "outer", split_axis=1, concat_axis=0, tiled=True)
    context = lax.all_gather(context, "outer", axis=0, tiled=True)
    weight_grad = lax.dot_general(context, owner_cols, (((0,), (0,)), ((), ())), preferred_element_type=F32)
    return (context_grad.astype(BF16), weight_grad * scale)


def solution(mesh):
    in_specs = (P("outer", "node"), P("outer", "node"), P("node", "outer"))
    out_specs = (P("outer", "node"), P("node", "outer"))
    return jax.shard_map(body, mesh=mesh, in_specs=in_specs, out_specs=out_specs, check_vma=False)
```

```python
import functools
import math

import jax
import jax.numpy as jnp
from jax import lax
from jax.experimental import pallas as pl
from jax.experimental.pallas import tpu as pltpu
from jax.sharding import PartitionSpec as P

F32, BF16 = jnp.float32, jnp.bfloat16
VMEM = pl.BlockSpec(memory_space=pltpu.VMEM)


def plane_of(outer):
    cores = 2 if outer % 2 == 0 else 1
    chips = outer // cores
    cols = max(d for d in range(1, math.isqrt(chips) + 1) if chips % d == 0)
    return chips // cols, cols, cores


def place(o, db, da, dc):
    rows, cols, cores = plane_of(lax.axis_size("outer"))
    b, a, c = o // (cols * cores), o // cores % cols, o % cores
    return ((b + db) % rows * cols + (a + da) % cols) * cores + (c + dc) % cores


def chip_at(db, da):
    rows, cols, cores = plane_of(lax.axis_size("outer"))
    chip = lax.div(lax.axis_index("outer"), jnp.int32(cores))
    b, a = lax.div(chip, jnp.int32(cols)), lax.rem(chip, jnp.int32(cols))
    return lax.rem(b + db % rows, jnp.int32(rows)) * cols + lax.rem(a + da % cols, jnp.int32(cols))


def kind_at(dc):
    cores = plane_of(lax.axis_size("outer"))[2]
    return lax.rem(lax.axis_index("outer") + dc, jnp.int32(cores))


def shift(array, db, da, dc=0):
    return lax.ppermute(array, "outer", [(place(o, db, da, dc), o) for o in range(lax.axis_size("outer"))])


def sibling(array, cuts=()):
    at = [0] + [int(array.shape[0] * cut) for cut in cuts] + [array.shape[0]]
    pieces = [shift(array[i:j], 0, 0, 1) for i, j in zip(at, at[1:])]
    return pieces[0] if len(pieces) == 1 else jnp.concatenate(pieces)


def along_node(array, d):
    node = lax.axis_size("node")
    return lax.ppermute(array, "node", [((i + d) % node, i) for i in range(node)])


def after(arrays, done):
    return lax.optimization_barrier((arrays, done))[0]


def call(kernel, out, *args, scratch=(), out_specs=None):
    return pl.pallas_call(
        kernel,
        out_shape=out,
        in_specs=[VMEM] * len(args),
        out_specs=out_specs or jax.tree.map(lambda _: VMEM, out),
        scratch_shapes=scratch,
        compiler_params=pltpu.CompilerParams(vmem_limit_bytes=40 * 2**20),
    )(*args)


class Sizes:
    def __init__(self, context, grad_out, out_weight):
        self.outer, self.node = lax.axis_size("outer"), lax.axis_size("node")
        self.rows, self.cols, self.cores = plane_of(self.outer)
        self.chips = self.rows * self.cols
        self.tokens, self.held = grad_out.shape
        self.taken, self.width = out_weight.shape
        self.row = [(0, da) for da in range(1, self.cols)]
        self.column = [(db, 0) for db in range(1, self.rows)]
        self.across = [(db, da) for db in range(1, self.rows) for da in range(1, self.cols)]
        self.half = self.taken // 2
        whole = self.held % (self.width * self.cores) == 0 and self.node % 2 == 0 and self.node > 2
        self.fits = whole and self.width % 128 == 0 and self.tokens % 128 == 0 and self.taken % 256 == 0


def route_kernel(s, *refs):
    blocks, (mine, other, whole) = refs[: s.node], refs[s.node :]
    for d, block in enumerate(blocks):
        whole[lax.rem(lax.axis_index("node") + d, jnp.int32(s.node))] = block[...]
    for out, kind in ((mine, kind_at(0)), (other, kind_at(1))):
        for chip in range(s.chips):
            first = chip * s.cores * s.width
            at = pl.multiple_of(first % s.held + kind * s.width, 128)
            out[chip] = whole[first // s.held, :, pl.ds(at, s.width)]


def pick_kernel(s, mine, theirs, *sent):
    odd = lax.rem(lax.axis_index("node"), jnp.int32(2))
    for (db, da), out in zip(s.row + s.column, sent):
        out[: s.tokens] = mine[chip_at(-db, -da)]
        out[s.tokens :] = theirs[chip_at(-db, -da)]
    for source, here in ((mine, odd == 0), (theirs, odd == 1)):

        @pl.when(here)
        def _(source=source):
            for (db, da), out in zip(s.across, sent[len(s.row + s.column) :]):
                out[...] = source[chip_at(-db, -da)]


def put(s, packed, slot, n, share, second):
    odd = lax.rem(lax.axis_index("node"), jnp.int32(2))
    for block, half in ((share, odd), (second, 1 - odd)):
        at = pl.multiple_of((half * n + slot) * s.tokens, 128)
        packed[pl.ds(at, s.tokens)] = block[...]


def turn_kernel(s, *refs):
    *blocks, out = refs
    at = 0
    for block in blocks:
        out[:, at : at + block.shape[0]] = block[...].T
        at += block.shape[0]


def over_chips(s, mine, theirs, pieces):
    total = 0.0
    for at, piece in pieces:
        chip = chip_at(*at)
        left = jnp.concatenate([mine[chip], theirs[chip]], axis=0)
        total += lax.dot_general(left, piece, (((1,), (1,)), ((), ())), preferred_element_type=F32)
    return total


def context_kernel(s, mine, theirs, *refs):
    *weights, out = refs
    for h in range(2):
        side = slice(h * s.half, (h + 1) * s.half)
        pieces = [(at, weight[side]) for at, weight in zip([(0, 0)] + s.row + s.column, weights)]
        out[:, side] = over_chips(s, mine, theirs, pieces)


def context_far_kernel(s, mine, theirs, near, *refs):
    *pairs, own, others = refs
    for h in range(2):
        side = slice(h * s.half, (h + 1) * s.half)
        total = near[:, side] + over_chips(s, mine, theirs, [(at, pairs[2 * k + h][...]) for k, at in enumerate(s.across)])
        own[:, side] = total[: s.tokens]
        others[:, side] = total[s.tokens :]


def blocks_of(rows, count=4):
    return [slice(i * rows // count, (i + 1) * rows // count) for i in range(count)]


def early_kernel(s, turned, theirs, far, far_theirs, mine, other, *refs):
    *blocks, out, packed = refs
    n = 1 + len(blocks) // 2
    packed[: s.tokens] = mine[chip_at(0, 0)]
    packed[n * s.tokens : (n + 1) * s.tokens] = other[chip_at(0, 0)]
    for k in range(1, n):
        put(s, packed, k, n, *blocks[2 * k - 2 : 2 * k])
    for rows in blocks_of(s.taken):
        left = [turned[rows, : s.tokens], far[rows], theirs[rows, : s.tokens], far_theirs[rows]]
        out[rows] = jnp.dot(jnp.concatenate(left, axis=1), packed[...], preferred_element_type=F32)


def add_kernel(s, k, sums, turned, theirs, block, out):
    at = slice((1 + k) * s.tokens, (2 + k) * s.tokens)
    for rows in blocks_of(s.taken):
        left = jnp.concatenate([turned[rows, at], theirs[rows, at]], axis=1)
        out[rows] = sums[rows] + jnp.dot(left, block[...], preferred_element_type=F32)


def last_kernel(s, scale, k, sums, turned, theirs, block, out, done, sems):
    at = slice((1 + k) * s.tokens, (2 + k) * s.tokens)
    copies = []
    for i, rows in enumerate(blocks_of(s.taken, sems.shape[0])):
        left = jnp.concatenate([turned[rows, at], theirs[rows, at]], axis=1)
        done[rows] = (sums[rows] + jnp.dot(left, block[...], preferred_element_type=F32)) * scale
        copies.append(pltpu.make_async_copy(done.at[rows], out.at[rows], sems.at[i]))
        copies[-1].start()
    for copy in copies:
        copy.wait()


def body(context, grad_out, out_weight):
    s = Sizes(context, grad_out, out_weight)
    if not s.fits or s.cores == 1:
        return plain(context, grad_out, out_weight)
    shape = lambda *dims, dtype=BF16: jax.ShapeDtypeStruct(dims, dtype)
    scale = 1.0 / math.sqrt(s.tokens * s.outer)
    near = s.row + s.column

    def straight(block):
        return {at: shift(block, *at) for at in near}

    def diagonal(blocks):
        half = next(iter(blocks.values())).shape[0] // 2
        pairs = []
        for db, da in s.across:
            pairs.append(shift(blocks[0, da][:half], db, 0))
            pairs.append(shift(blocks[db, 0][half:], 0, da))
        return pairs

    weights = straight(out_weight)
    around = {0: grad_out, s.node - 1: along_node(grad_out, -1), 1: along_node(grad_out, 1)}
    contexts = {at: shift(context, *at) for at in s.row}
    contexts |= {at: shift(after(context, around[s.node - 1]), *at) for at in s.column}
    weights, around = lax.optimization_barrier((weights, around))
    for step in range(2, s.node // 2 + 1):
        around[s.node - step] = along_node(around[s.node - step + 1], -1)
        if 2 * step < s.node:
            around[step] = along_node(around[step - 1], 1)
    weights_far = diagonal(weights)
    contexts_far = diagonal(contexts)
    turn = functools.partial(turn_kernel, s)
    turned = call(turn, shape(s.taken, (1 + len(near)) * s.tokens), context, *contexts.values())
    turned_other = sibling(turned)
    turned_far = call(turn, shape(s.taken, len(s.across) * s.tokens), *contexts_far)
    turned_far_other = sibling(turned_far)

    columns = shape(s.chips, s.tokens, s.width)
    mine, other = call(
        functools.partial(route_kernel, s), [columns] * 2, *[around[d] for d in range(s.node)],
        scratch=[pltpu.VMEM((s.node, s.tokens, s.held), BF16)],
    )
    theirs = sibling(after(other, weights_far))

    outs = [shape(s.cores * s.tokens, s.width)] * len(near) + [shape(s.tokens, s.width)] * len(s.across)
    sent = call(functools.partial(pick_kernel, s), outs, mine, after(theirs, turned_other))
    shares = [shift(x, *at) for x, at in zip(sent[len(near) :], s.across)]
    blocks = [shift(x, *at) for x, at in zip(sent, near)]
    far = [(x, lax.ppermute(x, "node", [(i ^ 1, i) for i in range(s.node)])) for x in shares]

    half_sums = shape(s.tokens, s.taken, dtype=F32)
    near_sums = call(
        functools.partial(context_kernel, s), shape(s.cores * s.tokens, s.taken, dtype=F32),
        mine, theirs, out_weight, *after([*weights.values()], turned_other),
    )
    own, others = call(functools.partial(context_far_kernel, s), [half_sums] * 2, mine, theirs, near_sums, *weights_far)
    context_grad = (own + sibling(others, (0.4375, 0.875))).astype(BF16)

    result = shape(s.taken, s.width, dtype=F32)
    sums = call(
        functools.partial(early_kernel, s), result,
        turned, turned_other, turned_far, turned_far_other, mine, theirs, *[x for two in far for x in two],
        scratch=[pltpu.VMEM((2 * (1 + len(far)) * s.tokens, s.width), BF16)],
    )
    for k, block in enumerate(blocks[:-1]):
        sums = call(functools.partial(add_kernel, s, k), result, sums, turned, turned_other, block)
    weight_grad = call(
        functools.partial(last_kernel, s, scale, len(blocks) - 1), result, sums, turned, turned_other, blocks[-1],
        out_specs=pl.BlockSpec(memory_space=pl.ANY),
        scratch=[pltpu.VMEM((s.taken, s.width), F32), pltpu.SemaphoreType.DMA((8,))],
    )
    return (context_grad, weight_grad)


def plain(context, grad_out, out_weight):
    grad_full = lax.all_gather(grad_out, "node", axis=1, tiled=True)
    weight = lax.all_gather(out_weight, "outer", axis=1, tiled=True)
    context_grad = lax.dot_general(grad_full, weight, (((1,), (1,)), ((), ())), preferred_element_type=F32)
    scale = 1.0 / math.sqrt(grad_full.shape[0] * lax.axis_size("outer"))
    owner_cols = lax.all_to_all(grad_full, "outer", split_axis=1, concat_axis=0, tiled=True)
    context = lax.all_gather(context, "outer", axis=0, tiled=True)
    weight_grad = lax.dot_general(context, owner_cols, (((0,), (0,)), ((), ())), preferred_element_type=F32)
    return (context_grad.astype(BF16), weight_grad * scale)


def solution(mesh):
    in_specs = (P("outer", "node"), P("outer", "node"), P("node", "outer"))
    out_specs = (P("outer", "node"), P("node", "outer"))
    return jax.shard_map(body, mesh=mesh, in_specs=in_specs, out_specs=out_specs, check_vma=False)
```

```python
import functools
import math

import jax
import jax.numpy as jnp
from jax import lax
from jax.experimental import pallas as pl
from jax.experimental.pallas import tpu as pltpu
from jax.sharding import PartitionSpec as P

F32, BF16 = jnp.float32, jnp.bfloat16
VMEM = pl.BlockSpec(memory_space=pltpu.VMEM)


def plane_of(outer):
    cores = 2 if outer % 2 == 0 else 1
    chips = outer // cores
    cols = max(d for d in range(1, math.isqrt(chips) + 1) if chips % d == 0)
    return chips // cols, cols, cores


def place(o, db, da, dc):
    rows, cols, cores = plane_of(lax.axis_size("outer"))
    b, a, c = o // (cols * cores), o // cores % cols, o % cores
    return ((b + db) % rows * cols + (a + da) % cols) * cores + (c + dc) % cores


def chip_at(db, da):
    rows, cols, cores = plane_of(lax.axis_size("outer"))
    chip = lax.div(lax.axis_index("outer"), jnp.int32(cores))
    b, a = lax.div(chip, jnp.int32(cols)), lax.rem(chip, jnp.int32(cols))
    return lax.rem(b + db % rows, jnp.int32(rows)) * cols + lax.rem(a + da % cols, jnp.int32(cols))


def kind_at(dc):
    cores = plane_of(lax.axis_size("outer"))[2]
    return lax.rem(lax.axis_index("outer") + dc, jnp.int32(cores))


def shift(array, db, da, dc=0):
    return lax.ppermute(array, "outer", [(place(o, db, da, dc), o) for o in range(lax.axis_size("outer"))])


def sibling(array, cuts=()):
    at = [0] + [int(array.shape[0] * cut) for cut in cuts] + [array.shape[0]]
    pieces = [shift(array[i:j], 0, 0, 1) for i, j in zip(at, at[1:])]
    return pieces[0] if len(pieces) == 1 else jnp.concatenate(pieces)


def along_node(array, d):
    node = lax.axis_size("node")
    return lax.ppermute(array, "node", [((i + d) % node, i) for i in range(node)])


def after(arrays, done):
    return lax.optimization_barrier((arrays, done))[0]


def call(kernel, out, *args, scratch=(), out_specs=None):
    return pl.pallas_call(
        kernel,
        out_shape=out,
        in_specs=[VMEM] * len(args),
        out_specs=out_specs or jax.tree.map(lambda _: VMEM, out),
        scratch_shapes=scratch,
        compiler_params=pltpu.CompilerParams(vmem_limit_bytes=40 * 2**20),
    )(*args)


class Sizes:
    def __init__(self, context, grad_out, out_weight):
        self.outer, self.node = lax.axis_size("outer"), lax.axis_size("node")
        self.rows, self.cols, self.cores = plane_of(self.outer)
        self.chips = self.rows * self.cols
        self.tokens, self.held = grad_out.shape
        self.taken, self.width = out_weight.shape
        self.row = [(0, da) for da in range(1, self.cols)]
        self.column = [(db, 0) for db in range(1, self.rows)]
        self.across = [(db, da) for db in range(1, self.rows) for da in range(1, self.cols)]
        self.half = self.taken // 2
        whole = self.held % (self.width * self.cores) == 0 and self.node % 2 == 0 and self.node > 2
        self.fits = whole and self.width % 128 == 0 and self.tokens % 128 == 0 and self.taken % 256 == 0


def route_kernel(s, *refs):
    blocks, (mine, other, whole) = refs[: s.node], refs[s.node :]
    for d, block in enumerate(blocks):
        whole[lax.rem(lax.axis_index("node") + d, jnp.int32(s.node))] = block[...]
    for out, kind in ((mine, kind_at(0)), (other, kind_at(1))):
        for chip in range(s.chips):
            first = chip * s.cores * s.width
            at = pl.multiple_of(first % s.held + kind * s.width, 128)
            out[chip] = whole[first // s.held, :, pl.ds(at, s.width)]


def pick_kernel(s, mine, theirs, *sent):
    odd = lax.rem(lax.axis_index("node"), jnp.int32(2))
    for (db, da), out in zip(s.row + s.column, sent):
        out[: s.tokens] = mine[chip_at(-db, -da)]
        out[s.tokens :] = theirs[chip_at(-db, -da)]
    for source, here in ((mine, odd == 0), (theirs, odd == 1)):

        @pl.when(here)
        def _(source=source):
            for (db, da), out in zip(s.across, sent[len(s.row + s.column) :]):
                out[...] = source[chip_at(-db, -da)]


def put(s, packed, slot, n, share, second):
    odd = lax.rem(lax.axis_index("node"), jnp.int32(2))
    for block, half in ((share, odd), (second, 1 - odd)):
        at = pl.multiple_of((half * n + slot) * s.tokens, 128)
        packed[pl.ds(at, s.tokens)] = block[...]


def turn_kernel(s, *refs):
    *blocks, out = refs
    at = 0
    for block in blocks:
        out[:, at : at + block.shape[0]] = block[...].T
        at += block.shape[0]


def over_chips(s, mine, theirs, pieces):
    total = 0.0
    for at, piece in pieces:
        chip = chip_at(*at)
        left = jnp.concatenate([mine[chip], theirs[chip]], axis=0)
        total += lax.dot_general(left, piece, (((1,), (1,)), ((), ())), preferred_element_type=F32)
    return total


def context_kernel(s, mine, theirs, *refs):
    *weights, out = refs
    for h in range(2):
        side = slice(h * s.half, (h + 1) * s.half)
        pieces = [(at, weight[side]) for at, weight in zip([(0, 0)] + s.row + s.column, weights)]
        out[:, side] = over_chips(s, mine, theirs, pieces)


def context_far_kernel(s, mine, theirs, near, *refs):
    *pairs, own, others = refs
    for h in range(2):
        side = slice(h * s.half, (h + 1) * s.half)
        total = near[:, side] + over_chips(s, mine, theirs, [(at, pairs[2 * k + h][...]) for k, at in enumerate(s.across)])
        own[:, side] = total[: s.tokens]
        others[:, side] = total[s.tokens :]


def blocks_of(rows):
    return [slice(i * rows // 4, (i + 1) * rows // 4) for i in range(4)]


def early_kernel(s, turned, theirs, far, far_theirs, mine, other, *refs):
    *blocks, out, packed = refs
    n = 1 + len(blocks) // 2
    packed[: s.tokens] = mine[chip_at(0, 0)]
    packed[n * s.tokens : (n + 1) * s.tokens] = other[chip_at(0, 0)]
    for k in range(1, n):
        put(s, packed, k, n, *blocks[2 * k - 2 : 2 * k])
    for rows in blocks_of(s.taken):
        left = [turned[rows, : s.tokens], far[rows], theirs[rows, : s.tokens], far_theirs[rows]]
        out[rows] = jnp.dot(jnp.concatenate(left, axis=1), packed[...], preferred_element_type=F32)


def add_kernel(s, k, sums, turned, theirs, block, out):
    at = slice((1 + k) * s.tokens, (2 + k) * s.tokens)
    for rows in blocks_of(s.taken):
        left = jnp.concatenate([turned[rows, at], theirs[rows, at]], axis=1)
        out[rows] = sums[rows] + jnp.dot(left, block[...], preferred_element_type=F32)


def last_kernel(s, scale, k, sums, turned, theirs, block, out, done, sems):
    at = slice((1 + k) * s.tokens, (2 + k) * s.tokens)
    copies = []
    for i, rows in enumerate(blocks_of(s.taken)):
        left = jnp.concatenate([turned[rows, at], theirs[rows, at]], axis=1)
        done[rows] = (sums[rows] + jnp.dot(left, block[...], preferred_element_type=F32)) * scale
        copies.append(pltpu.make_async_copy(done.at[rows], out.at[rows], sems.at[i]))
        copies[-1].start()
    for copy in copies:
        copy.wait()


def body(context, grad_out, out_weight):
    s = Sizes(context, grad_out, out_weight)
    if not s.fits or s.cores == 1:
        return plain(context, grad_out, out_weight)
    shape = lambda *dims, dtype=BF16: jax.ShapeDtypeStruct(dims, dtype)
    scale = 1.0 / math.sqrt(s.tokens * s.outer)
    near = s.row + s.column

    def straight(block):
        return {at: shift(block, *at) for at in near}

    def diagonal(blocks):
        half = next(iter(blocks.values())).shape[0] // 2
        pairs = []
        for db, da in s.across:
            pairs.append(shift(blocks[0, da][:half], db, 0))
            pairs.append(shift(blocks[db, 0][half:], 0, da))
        return pairs

    weights = straight(out_weight)
    around = {0: grad_out, s.node - 1: along_node(grad_out, -1), 1: along_node(grad_out, 1)}
    contexts = {at: shift(context, *at) for at in s.row}
    contexts |= {at: shift(after(context, around[s.node - 1]), *at) for at in s.column}
    weights, around = lax.optimization_barrier((weights, around))
    for step in range(2, s.node // 2 + 1):
        around[s.node - step] = along_node(around[s.node - step + 1], -1)
        if 2 * step < s.node:
            around[step] = along_node(around[step - 1], 1)
    weights_far = diagonal(weights)
    contexts_far = diagonal(contexts)
    turn = functools.partial(turn_kernel, s)
    turned = call(turn, shape(s.taken, (1 + len(near)) * s.tokens), context, *contexts.values())
    turned_other = sibling(turned)
    turned_far = call(turn, shape(s.taken, len(s.across) * s.tokens), *contexts_far)
    turned_far_other = sibling(turned_far)

    columns = shape(s.chips, s.tokens, s.width)
    mine, other = call(
        functools.partial(route_kernel, s), [columns] * 2, *[around[d] for d in range(s.node)],
        scratch=[pltpu.VMEM((s.node, s.tokens, s.held), BF16)],
    )
    theirs = sibling(after(other, weights_far))

    outs = [shape(s.cores * s.tokens, s.width)] * len(near) + [shape(s.tokens, s.width)] * len(s.across)
    sent = call(functools.partial(pick_kernel, s), outs, mine, after(theirs, turned_other))
    shares = [shift(x, *at) for x, at in zip(sent[len(near) :], s.across)]
    blocks = [shift(x, *at) for x, at in zip(sent, near)]
    far = [(x, lax.ppermute(x, "node", [(i ^ 1, i) for i in range(s.node)])) for x in shares]

    half_sums = shape(s.tokens, s.taken, dtype=F32)
    near_sums = call(
        functools.partial(context_kernel, s), shape(s.cores * s.tokens, s.taken, dtype=F32),
        mine, theirs, out_weight, *after([*weights.values()], turned_other),
    )
    own, others = call(functools.partial(context_far_kernel, s), [half_sums] * 2, mine, theirs, near_sums, *weights_far)
    context_grad = (own + sibling(others, (0.375, 0.59375))).astype(BF16)

    result = shape(s.taken, s.width, dtype=F32)
    sums = call(
        functools.partial(early_kernel, s), result,
        turned, turned_other, turned_far, turned_far_other, mine, theirs, *[x for two in far for x in two],
        scratch=[pltpu.VMEM((2 * (1 + len(far)) * s.tokens, s.width), BF16)],
    )
    for k, block in enumerate(blocks[:-1]):
        sums = call(functools.partial(add_kernel, s, k), result, sums, turned, turned_other, block)
    weight_grad = call(
        functools.partial(last_kernel, s, scale, len(blocks) - 1), result, sums, turned, turned_other, blocks[-1],
        out_specs=pl.BlockSpec(memory_space=pl.ANY),
        scratch=[pltpu.VMEM((s.taken, s.width), F32), pltpu.SemaphoreType.DMA((4,))],
    )
    return (context_grad, weight_grad)


def plain(context, grad_out, out_weight):
    grad_full = lax.all_gather(grad_out, "node", axis=1, tiled=True)
    weight = lax.all_gather(out_weight, "outer", axis=1, tiled=True)
    context_grad = lax.dot_general(grad_full, weight, (((1,), (1,)), ((), ())), preferred_element_type=F32)
    scale = 1.0 / math.sqrt(grad_full.shape[0] * lax.axis_size("outer"))
    owner_cols = lax.all_to_all(grad_full, "outer", split_axis=1, concat_axis=0, tiled=True)
    context = lax.all_gather(context, "outer", axis=0, tiled=True)
    weight_grad = lax.dot_general(context, owner_cols, (((0,), (0,)), ((), ())), preferred_element_type=F32)
    return (context_grad.astype(BF16), weight_grad * scale)


def solution(mesh):
    in_specs = (P("outer", "node"), P("outer", "node"), P("node", "outer"))
    out_specs = (P("outer", "node"), P("node", "outer"))
    return jax.shard_map(body, mesh=mesh, in_specs=in_specs, out_specs=out_specs, check_vma=False)
```
